256 devices in a mesh: br: 64 (over z, y, core), hd: 4 (over x).
Axes of the slice: x: 4, y: 4, z: 8, core: 2. Of those that a mesh axis runs over, the one named last changes fastest.
Arguments:
- branch_q: bfloat16 [32768, 5120], P('br', 'hd'), may hold values from -600 to 600
- branch_k: bfloat16 [32768, 5120], P('br', 'hd'), may hold values from -6 to 6
- branch_v: bfloat16 [32768, 5120], P('br', 'hd'), may hold values from -6 to 6
- branch_out: bfloat16 [32768, 5120], P('br', 'hd'), may hold values from -6 to 6
- branch_grad: bfloat16 [32768, 5120], P('br', 'hd'), may hold values from -6 to 6
- prefix_k: bfloat16 [2, 256, 5120], P(None, 'hd'), may hold values from -6 to 6
- prefix_v: bfloat16 [2, 256, 5120], P(None, 'hd'), may hold values from -6 to 6
- parents: int32 [64, 4], P('br'), may hold values from -1 to 2, as said below
- lengths: int32 [64, 4], P('br'), may hold values from 1 to 128, as said below
- prompt_of: int32 [64, 1], replicated, may hold values from 0 to 1
Outputs:
- branch_dq: bfloat16 [32768, 5120], P('br', 'hd')
- branch_dk: bfloat16 [32768, 5120], P('br', 'hd')
- branch_dv: bfloat16 [32768, 5120], P('br', 'hd')
- prefix_dk: bfloat16 [2, 256, 5120], P(None, 'hd')
- prefix_dv: bfloat16 [2, 256, 5120], P(None, 'hd')
The draws below stay inside these ranges and needn't reach their ends.
Inputs may be any that keep to these rules, and one draw needn't show every extreme that they name: `parents`: every parent is below its own block; each tree's last block has the block before it as parent. `lengths`: each tree's first block is full; the first tree's last block holds one token.
All inputs are finite; a program needn't handle non-finite values.
Results may differ from the reference program's by a relative error of at most 0.0075.
Values may be sent and summed in bfloat16 or wider, within the bound.
A program may use at most 128 MiB of HBM per device.

```python
import jax
import jax.numpy as jnp
from jax import lax

D = 5120
HS = 128
TILE = 128
BLOCKS = 4
PLEN = 256
PROMPTS = 2
ROWS_DEV = 512
TREES = 64
BR_ROWS = 32768


def shared_field(key):
    return jnp.clip(jax.random.normal(key, (BR_ROWS, D), jnp.float32), -6.0, 6.0)


def draw_branch_k(key, part):
    field = shared_field(key)
    return field.astype(jnp.bfloat16)


def draw_branch_q(key, part):
    key = jax.random.fold_in(key, 5)
    return jnp.clip(jax.random.normal(key, (BR_ROWS, D), jnp.float32), -6.0, 6.0).astype(jnp.bfloat16)


def draw_branch_out(key, part):
    key = jax.random.fold_in(key, 13)
    return jnp.clip(jax.random.normal(key, (BR_ROWS, D), jnp.float32), -6.0, 6.0).astype(jnp.bfloat16)


def draw_branch_grad(key, part):
    key = jax.random.fold_in(key, 17)
    return jnp.clip(jax.random.normal(key, (BR_ROWS, D), jnp.float32), -6.0, 6.0).astype(jnp.bfloat16)


def draw_prefix_k(key, part):
    key = jax.random.fold_in(key, 19)
    return jnp.clip(jax.random.normal(key, (PROMPTS, PLEN, D), jnp.float32), -6.0, 6.0).astype(jnp.bfloat16)


def draw_prefix_v(key, part):
    key = jax.random.fold_in(key, 23)
    return jnp.clip(jax.random.normal(key, (PROMPTS, PLEN, D), jnp.float32), -6.0, 6.0).astype(jnp.bfloat16)


def draw_parents(key, part):
    key = jax.random.fold_in(key, 3)
    upper = jnp.arange(BLOCKS, dtype=jnp.int32)[None, :]
    chosen = jax.random.randint(key, (TREES, BLOCKS), -1, jnp.maximum(upper, 0))
    return chosen.at[:, BLOCKS - 1].set(BLOCKS - 2)


def draw_lengths(key, part):
    key = jax.random.fold_in(key, 7)
    counts = jax.random.randint(key, (TREES, BLOCKS), 1, TILE + 1)
    counts = counts.at[:, 0].set(TILE)
    return counts.at[0, BLOCKS - 1].set(1)


def level_of(stream_key, shape, split, least, high):
    level = 1.0
    for dim, blocks in split:
        draws = jax.random.uniform(jax.random.fold_in(jax.random.fold_in(stream_key, 6), dim), (blocks,), jnp.float32, least / len(split), high / len(split))
        level = level * jnp.repeat(jnp.exp(draws), shape[dim] // blocks).reshape((-1,) + (1,) * (len(shape) - 1 - dim))
    return level


def choose_distinct(key, rows, amount, top, lift):
    order = jax.random.permutation(jax.random.fold_in(key, 1), amount)
    favour = order
    for power in range(3):
        favour = favour * favour // amount
    favour = favour * lift // amount
    chance = jax.random.randint(jax.random.fold_in(key, 2), (rows, amount), 0, 4096) + favour
    sure = jax.random.permutation(jax.random.fold_in(key, 3), rows)[jnp.arange(amount) % rows]
    chance = jnp.where(jnp.arange(rows)[:, None] == sure[None, :], 1 << 14, chance)
    merit = chance * amount + jnp.arange(amount)
    return lax.top_k(merit.astype(jnp.int32), top)[1].astype(jnp.int32)


def gaussian(stream_key, shape, width, most, pieces=(), held_as=jnp.bfloat16):
    loudness = level_of(stream_key, shape, pieces, -0.22, 0.18) if pieces else 1.0
    entries = jax.random.normal(stream_key, shape, jnp.float32) * width * loudness
    return jnp.minimum(jnp.maximum(entries, -most), most).astype(held_as)


def setup_inputs(seed: int = 0) -> dict:
    key_of = jax.random.split(jax.random.key(seed), 11)
    branch_q = draw_branch_q(jax.random.fold_in(key_of[10], 71), 0)
    branch_k = draw_branch_k(jax.random.fold_in(key_of[10], 71), 0)
    branch_v = gaussian(key_of[2], (BR_ROWS, D), 1.0, 6.0, ((0, 64), (1, 4)))
    branch_out = draw_branch_out(jax.random.fold_in(key_of[10], 71), 0)
    branch_grad = draw_branch_grad(jax.random.fold_in(key_of[10], 71), 0)
    prefix_k = draw_prefix_k(jax.random.fold_in(key_of[10], 71), 0)
    prefix_v = draw_prefix_v(jax.random.fold_in(key_of[10], 71), 0)
    parents = draw_parents(jax.random.fold_in(key_of[10], 71), 0)
    lengths = draw_lengths(jax.random.fold_in(key_of[10], 71), 0)
    prompt_of = choose_distinct(key_of[9], TREES, PROMPTS, 1, 0)
    return dict(branch_q=branch_q, branch_k=branch_k, branch_v=branch_v, branch_out=branch_out, branch_grad=branch_grad, prefix_k=prefix_k, prefix_v=prefix_v, parents=parents, lengths=lengths, prompt_of=prompt_of)


neg_fill = -1.0e30


def ancestors(parents, blocks):
    block_ids = jnp.arange(blocks, dtype=jnp.int32)
    parent_hit = parents[:, None] == block_ids[None, :]

    def extend(sweep_num, found_set):
        return found_set | jnp.any(found_set[:, :, None] & parent_hit[None, :, :], axis=1)

    return lax.fori_loop(0, blocks, extend, parent_hit)


def tree_masks(parents, lengths, tile_rows, prefix_len):
    blocks = parents.shape[0]
    ancestor = ancestors(parents, blocks)
    row_count = blocks * tile_rows
    row_index = jnp.arange(row_count, dtype=jnp.int32)
    block_of = row_index // tile_rows
    offset = row_index % tile_rows
    fill_count = jnp.repeat(lengths, tile_rows)
    live_rows = offset < fill_count
    same_block = block_of[:, None] == block_of[None, :]
    earlier = offset[None, :] <= offset[:, None]
    wide_above = jnp.repeat(jnp.repeat(ancestor, tile_rows, axis=0), tile_rows, axis=1)
    allowed = live_rows[None, :] & (wide_above | (same_block & earlier))
    full_mask = jnp.concatenate([jnp.ones((row_count, prefix_len), dtype=bool), allowed], axis=1)
    return full_mask, live_rows


def head_grads(queries, key_rows, value_rows, output, cotangent, full_mask, live_rows, scaling):
    scores = jnp.dot(queries, key_rows.T, preferred_element_type=jnp.float32) * scaling
    scores = jnp.where(full_mask, scores, neg_fill)
    row_max = jnp.max(scores, axis=1, keepdims=True)
    shifted = jnp.exp(scores - row_max)
    attention = shifted / jnp.sum(shifted, axis=1, keepdims=True)
    attention_low = attention.astype(jnp.bfloat16)
    kept_grad = jnp.where(live_rows[:, None], cotangent, jnp.zeros_like(cotangent))
    dvalues = jnp.dot(attention_low.T, kept_grad, preferred_element_type=jnp.float32)
    dattention = jnp.dot(kept_grad, value_rows.T, preferred_element_type=jnp.float32)
    row_dot = jnp.sum(kept_grad.astype(jnp.float32) * output.astype(jnp.float32), axis=1, keepdims=True)
    dscore = (attention * (dattention - row_dot)).astype(jnp.bfloat16)
    dquery = jnp.dot(dscore, key_rows, preferred_element_type=jnp.float32) * scaling
    dkey_rows = jnp.dot(dscore.T, queries, preferred_element_type=jnp.float32) * scaling
    return dquery, dkey_rows, dvalues


def tree_grads(queries, branch_keys, branch_values, output, cotangent, prompt_keys, prompt_values, parents, lengths, head_size, tile_rows):
    prefix_len = prompt_keys.shape[0]
    full_mask, live_rows = tree_masks(parents, lengths, tile_rows, prefix_len)
    all_keys = jnp.concatenate([prompt_keys, branch_keys], axis=0)
    all_values = jnp.concatenate([prompt_values, branch_values], axis=0)
    head_count = queries.shape[1] // head_size
    scaling = head_size ** -0.5
    row_count = queries.shape[0]
    key_total = all_keys.shape[0]
    columns = queries.shape[1]
    zeros_init = (jnp.zeros((row_count, columns), jnp.float32), jnp.zeros((key_total, columns), jnp.float32), jnp.zeros((key_total, columns), jnp.float32))

    def one_head(head_num, partial_value):
        col_start = head_num * head_size

        def slice_cols(array):
            return lax.dynamic_slice_in_dim(array, col_start, head_size, 1)

        dquery, dkey_rows, dvalues = head_grads(slice_cols(queries), slice_cols(all_keys), slice_cols(all_values), slice_cols(output), slice_cols(cotangent), full_mask, live_rows, scaling)
        return (lax.dynamic_update_slice_in_dim(partial_value[0], dquery, col_start, 1),
                lax.dynamic_update_slice_in_dim(partial_value[1], dkey_rows, col_start, 1),
                lax.dynamic_update_slice_in_dim(partial_value[2], dvalues, col_start, 1))

    dquery, dkey_rows, dvalues = lax.fori_loop(0, head_count, one_head, zeros_init)
    return (dquery.astype(jnp.bfloat16), dkey_rows[prefix_len:].astype(jnp.bfloat16), dvalues[prefix_len:].astype(jnp.bfloat16), dkey_rows[:prefix_len], dvalues[:prefix_len])


def reference(branch_q, branch_k, branch_v, branch_out, branch_grad, prefix_k, prefix_v, parents, lengths, prompt_of):
    owners = prompt_of[:, 0]

    def per_tree(sums, tree_num):
        row_start = tree_num * ROWS_DEV

        def slice_rows(array):
            return lax.dynamic_slice_in_dim(array, row_start, ROWS_DEV, 0)

        prompt_num = owners[tree_num]
        prompt_keys = lax.dynamic_index_in_dim(prefix_k, prompt_num, 0, keepdims=False)
        prompt_values = lax.dynamic_index_in_dim(prefix_v, prompt_num, 0, keepdims=False)
        tree_parents = lax.dynamic_index_in_dim(parents, tree_num, 0, keepdims=False)
        tree_lengths = lax.dynamic_index_in_dim(lengths, tree_num, 0, keepdims=False)
        dquery, dkey, dvalue, prompt_dk, prompt_dv = tree_grads(slice_rows(branch_q), slice_rows(branch_k), slice_rows(branch_v), slice_rows(branch_out), slice_rows(branch_grad), prompt_keys, prompt_values, tree_parents, tree_lengths, HS, TILE)
        sum_keys = sums[0].at[prompt_num].add(prompt_dk)
        sum_values = sums[1].at[prompt_num].add(prompt_dv)
        return (sum_keys, sum_values), (dquery, dkey, dvalue)

    start_sums = (jnp.zeros((PROMPTS, PLEN, D), jnp.float32), jnp.zeros((PROMPTS, PLEN, D), jnp.float32))
    (sum_keys, sum_values), (dquery, dkey, dvalue) = lax.scan(per_tree, start_sums, jnp.arange(TREES, dtype=jnp.int32))
    return (dquery.reshape(BR_ROWS, D), dkey.reshape(BR_ROWS, D), dvalue.reshape(BR_ROWS, D), sum_keys.astype(jnp.bfloat16), sum_values.astype(jnp.bfloat16))
```

```python
import functools

import jax
import jax.numpy as jnp
from jax import lax
from jax.experimental import pallas as pl
from jax.experimental.pallas import tpu as pltpu
from jax.sharding import PartitionSpec as P

HS = 128
TILE = 128
BLOCKS = 4
PLEN = 256
PROMPTS = 2
ROWS = 512
HEADS = 10
COLS = 1280
GROUPS = 4
NY = 4
NZ = 8
LOG2E = 1.4426950408889634
MESH = pl.DeviceIdType.MESH
VMEM = pltpu.VMEM
WIDTHS = (384, 256)
STARTS = (0, 768)


def place():
    br = lax.axis_index("br")
    core = br % 2
    y = (br // 2) % NY
    z = br // (2 * NY)
    return lax.axis_index("hd"), y, z, core


def device(x, y, z, core):
    return ((z * NY + y) * 2 + core, x)


def greet(partners):
    barrier = pltpu.get_barrier_semaphore()
    for who in partners:
        pl.semaphore_signal(barrier, inc=1, device_id=who, device_id_type=MESH)
    pl.semaphore_wait(barrier, len(partners))


def remote(src, dst, send, recv, who):
    return pltpu.make_async_remote_copy(
        src_ref=src, dst_ref=dst, send_sem=send, recv_sem=recv, device_id=who, device_id_type=MESH
    )


def gather_kernel(owner, pk, pv, out_k, out_v, held, send_sem, recv_sem):
    x, y, z, core = place()
    partners = [device((x + d) % GROUPS, y, z, core) for d in (1, 2, 3)]
    own = owner[lax.axis_index("br")]
    outs = (out_k, out_v)
    rows = pl.ds(pl.multiple_of(x * 64, 64), 64)
    for a, table in enumerate((pk, pv)):
        for g in range(GROUPS):
            held[a, g] = table[own, :, g * COLS : (g + 1) * COLS]
    greet(partners)
    copies = []
    for a in range(2):
        for d in (2, 1, 3):
            copies.append(
                remote(
                    held.at[a, (x + d) % GROUPS],
                    outs[a].at[rows],
                    send_sem.at[a, d - 1],
                    recv_sem.at[a, d - 1],
                    partners[d - 1],
                )
            )
            copies[-1].start()
    for a in range(2):
        outs[a][rows, :] = held[a, x]
    for copy in copies:
        copy.wait()


def gather_prefix(owners, prefix_k, prefix_v):
    own = jax.ShapeDtypeStruct((PLEN, COLS), jnp.bfloat16)
    spec = pl.BlockSpec(memory_space=VMEM)
    return pl.pallas_call(
        gather_kernel,
        out_shape=(own, own),
        in_specs=[pl.BlockSpec(memory_space=pltpu.SMEM), spec, spec],
        out_specs=(spec, spec),
        scratch_shapes=[
            VMEM((2, GROUPS, 64, COLS), jnp.bfloat16),
            pltpu.SemaphoreType.DMA((2, 3)),
            pltpu.SemaphoreType.DMA((2, 3)),
        ],
        compiler_params=pltpu.CompilerParams(
            collective_id=1, has_side_effects=True, vmem_limit_bytes=24 << 20
        ),
        name="gather_prefix",
    )(owners, prefix_k, prefix_v)


def dot(a, b):
    return jnp.dot(a, b, preferred_element_type=jnp.float32)


def dot_t(a, b):
    return lax.dot_general(a, b, (((1,), (1,)), ((), ())), preferred_element_type=jnp.float32)


def head_kernel(parents, lengths, q, k, v, o, g, pk, pv, dq, dk, dv, pdk, pdv, bias):
    @pl.when(pl.program_id(0) == 0)
    def _():
        key = lax.broadcasted_iota(jnp.int32, (TILE, TILE), 0)
        query = lax.broadcasted_iota(jnp.int32, (TILE, TILE), 1)
        reach = {}
        for b in range(BLOCKS):
            up = parents[0, b]
            for c in range(b):
                hit = (up == c).astype(jnp.int32)
                for mid in range(c + 1, b):
                    hit = hit | ((up == mid).astype(jnp.int32) & reach[mid, c])
                reach[b, c] = hit
        for c in range(BLOCKS):
            for b in range(BLOCKS):
                if b > c:
                    seen = key < reach[b, c] * lengths[0, c]
                elif b == c:
                    seen = (key < lengths[0, c]) & (key <= query)
                else:
                    seen = key < 0
                bias[c * TILE : (c + 1) * TILE, b * TILE : (b + 1) * TILE] = jnp.where(seen, 0.0, -1e30)

    scale = HS**-0.5
    row = lax.broadcasted_iota(jnp.int32, (TILE, HS), 0)
    live = [row < lengths[0, b] for b in range(BLOCKS)]
    pre_dk = pre_dv = None
    tree_dk, tree_dv = [None] * 2, [None] * 2
    pk_t = pk[...].T
    k_t = k[...].T
    for pair in range(2):
        rows = pl.ds(256 * pair, 256)
        known = 256 * (pair + 1)
        qp = q[rows, :]
        gp = jnp.concatenate(
            [jnp.where(live[b], g[b * TILE : (b + 1) * TILE, :], jnp.zeros((), g.dtype)) for b in (2 * pair, 2 * pair + 1)],
            axis=0,
        )
        spread = (gp.astype(jnp.float32) * o[rows, :].astype(jnp.float32)).T
        row_dot = jnp.sum(spread, axis=0, keepdims=True)
        s_pre = dot_t(pk[...], qp) * (scale * LOG2E)
        s_tree = dot_t(k[:known, :], qp) * (scale * LOG2E) + bias[:known, rows]
        top = jnp.maximum(jnp.max(s_pre, axis=0, keepdims=True), jnp.max(s_tree, axis=0, keepdims=True))
        e_pre = jnp.exp2(s_pre - top)
        e_tree = jnp.exp2(s_tree - top)
        total = jnp.sum(e_pre, axis=0, keepdims=True) + jnp.sum(e_tree, axis=0, keepdims=True)
        part = 1.0 / total
        a_pre = e_pre * part
        a_tree = e_tree * part
        ds_pre = (a_pre * (dot_t(pv[...], gp) - row_dot)).astype(jnp.bfloat16)
        ds_tree = (a_tree * (dot_t(v[:known, :], gp) - row_dot)).astype(jnp.bfloat16)
        a_pre = a_pre.astype(jnp.bfloat16)
        a_tree = a_tree.astype(jnp.bfloat16)
        got_dv, got_dk = dot(a_pre, gp), dot(ds_pre, qp)
        tree_v, tree_k = dot(a_tree, gp), dot(ds_tree, qp)
        dq_t = dot(pk_t, ds_pre) + dot(k_t[:, :known], ds_tree)
        dq[rows, :] = (dq_t.T * scale).astype(jnp.bfloat16)
        if pair == 0:
            pre_dk, pre_dv = got_dk, got_dv
            first_k, first_v = tree_k, tree_v
        else:
            pdk[...] = ((pre_dk + got_dk) * scale).astype(jnp.bfloat16)
            pdv[...] = (pre_dv + got_dv).astype(jnp.bfloat16)
            dk[:256, :] = ((first_k + tree_k[:256]) * scale).astype(jnp.bfloat16)
            dv[:256, :] = (first_v + tree_v[:256]).astype(jnp.bfloat16)
            dk[256:, :] = (tree_k[256:] * scale).astype(jnp.bfloat16)
            dv[256:, :] = tree_v[256:].astype(jnp.bfloat16)


def heads(parents, lengths, q, k, v, o, g, pk, pv):
    tree = pl.BlockSpec((ROWS, HS), lambda h: (0, h))
    pre = pl.BlockSpec((PLEN, HS), lambda h: (0, h))
    table = pl.BlockSpec(memory_space=pltpu.SMEM)
    big = jax.ShapeDtypeStruct((ROWS, COLS), jnp.bfloat16)
    small = jax.ShapeDtypeStruct((PLEN, COLS), jnp.bfloat16)
    return pl.pallas_call(
        head_kernel,
        grid=(HEADS,),
        out_shape=(big, big, big, small, small),
        in_specs=[table, table, tree, tree, tree, tree, tree, pre, pre],
        out_specs=(tree, tree, tree, pre, pre),
        scratch_shapes=[VMEM((ROWS, ROWS), jnp.float32)],
        compiler_params=pltpu.CompilerParams(vmem_limit_bytes=32 << 20),
        name="head_grads",
    )(parents, lengths, q, k, v, o, g, pk, pv)


def f32(value):
    return value.astype(jnp.float32)


def bf16(value):
    return value.astype(jnp.bfloat16)


def reduce_kernel(owner, dkp, dvp, out_k, out_v, *scratch):
    x, y, z, core = place()
    (other, part0, part1, line0, line1, got_y0, got_y1, got_z0, got_z1, all0, all1, swap0, swap1,
     core_send, core_recv, y_send, y_recv, z_send, z_recv, x_send, x_recv,
     ay_send, ay_recv, az_send, az_recv, end_send, end_recv) = scratch
    mate = device(x, y, z, 1 - core)
    y_peers = [device(x, (y + d) % NY, z, core) for d in range(1, NY)]
    z_peers = [device(x, y, (z + d) % NZ, core) for d in range(1, NZ)]
    x_peers = [device((x + d) % GROUPS, y, z, core) for d in range(1, GROUPS)]
    greet([mate] + y_peers + z_peers + x_peers)
    br = lax.axis_index("br")
    mine = owner[br]
    its = owner[br + 1 - 2 * core]
    outs = (out_k, out_v)
    sums = (dkp, dvp)

    def one_core(c, part, line, got_y, got_z, full):
        width, start = WIDTHS[c], STARTS[c]
        other_width, other_start = WIDTHS[1 - c], STARTS[1 - c]
        first = []
        for a in range(2):
            copy = remote(
                sums[a].at[:, pl.ds(other_start, 2 * other_width)],
                other.at[a, :, pl.ds(0, 2 * other_width)],
                core_send.at[a],
                core_recv.at[a],
                mate,
            )
            copy.start()
            back = remote(
                sums[a].at[:, pl.ds(start, 2 * width)],
                other.at[a, :, pl.ds(0, 2 * width)],
                core_send.at[a],
                core_recv.at[a],
                mate,
            )
            first.append((copy, back))
        weights = [
            ((mine == p).astype(jnp.float32), (its == p).astype(jnp.float32)) for p in range(PROMPTS)
        ]
        for a in range(2):
            first[a][0].wait_send()
            first[a][1].wait_recv()

            @pl.loop(0, 16)
            def _(tile, a=a):
                to, rt = tile // 4, tile % 4
                rows = pl.ds(pl.multiple_of(tile * 16, 16), 16)
                for half in range(2):
                    own = f32(sums[a][rows, start + half * width : start + (half + 1) * width])
                    its_rows = f32(other[a, rows, half * width : (half + 1) * width])
                    for p in range(PROMPTS):
                        part[2 * a + half, 4 * p + rt, to] = bf16(weights[p][0] * own + weights[p][1] * its_rows)

        def spread(axis_peers, me, count, block, landing, sends, recvs):
            copies = []
            for d in range(1, count):
                copy = remote(block((me + d) % count), landing.at[d - 1], sends.at[d - 1], recvs.at[d - 1], axis_peers[d - 1])
                copy.start()
                copies.append(copy)
            for copy in copies:
                copy.wait()

        if c == 0:
            spread(y_peers, y, NY, lambda t: part.at[t], got_y, y_send, y_recv)

            @pl.loop(0, NZ * GROUPS)
            def _(i):
                a, b = i // GROUPS, i % GROUPS
                total = f32(part[y, a, b])
                for d in range(NY - 1):
                    total += f32(got_y[d, a, b])
                line[a, b] = bf16(total)

            spread(z_peers, z, NZ, lambda t: line.at[t], got_z, z_send, z_recv)

            @pl.loop(0, GROUPS)
            def _(b):
                total = f32(line[z, b])
                for d in range(NZ - 1):
                    total += f32(got_z[d, b])
                line[z, b] = bf16(total)

            block = line.at[z]
        else:
            spread(z_peers, z, NZ, lambda t: part.at[:, t], got_z, z_send, z_recv)

            @pl.loop(0, NY * GROUPS)
            def _(i):
                a, b = i // GROUPS, i % GROUPS
                total = f32(part[a, z, b])
                for d in range(NZ - 1):
                    total += f32(got_z[d, a, b])
                line[a, b] = bf16(total)

            spread(y_peers, y, NY, lambda t: line.at[t], got_y, y_send, y_recv)

            @pl.loop(0, GROUPS)
            def _(b):
                total = f32(line[y, b])
                for d in range(NY - 1):
                    total += f32(got_y[d, b])
                line[y, b] = bf16(total)

            block = line.at[y]
        full[y, z, x] = block[x]
        copies = []
        for d in range(1, GROUPS):
            copy = remote(
                block.at[(x + d) % GROUPS], full.at[y, z, x], x_send.at[d - 1], x_recv.at[d - 1], x_peers[d - 1]
            )
            copy.start()
            copies.append(copy)
        for copy in copies:
            copy.wait()

        def share(axis_peers, ref, sends, recvs):
            copies = []
            for d in range(len(axis_peers)):
                copy = remote(ref, ref, sends.at[d], recvs.at[d], axis_peers[d])
                copy.start()
                copies.append(copy)
            for copy in copies:
                copy.wait()

        if c == 0:
            share(z_peers, full.at[y, z], az_send, az_recv)
            share(y_peers, full.at[y], ay_send, ay_recv)
        else:
            share(y_peers, full.at[y, z], ay_send, ay_recv)
            share(z_peers, full.at[:, z], az_send, az_recv)

    @pl.when(core == 0)
    def _():
        one_core(0, part0, line0, got_y0, got_z0, all0)
        copy = remote(all0, swap0, end_send.at[0], end_recv.at[0], mate)
        back = remote(all1, swap1, end_send.at[1], end_recv.at[1], mate)
        copy.start()
        copy.wait_send()
        back.wait_recv()

    @pl.when(core == 1)
    def _():
        one_core(1, part1, line1, got_y1, got_z1, all1)
        copy = remote(all1, swap1, end_send.at[1], end_recv.at[1], mate)
        back = remote(all0, swap0, end_send.at[0], end_recv.at[0], mate)
        copy.start()
        copy.wait_send()
        back.wait_recv()

    def place_all(sources):
        @pl.loop(0, NZ)
        def _(t):
            p, rt = t // 4, t % 4
            rows = pl.ds(pl.multiple_of(rt * 16, 16), 16)
            for c in range(2):
                for yy in range(NY):
                    for xx in range(GROUPS):
                        at = xx * COLS + STARTS[c] + (yy % 2) * WIDTHS[c]
                        outs[yy // 2][p, rows, at : at + WIDTHS[c]] = sources[c][yy, t, xx]

    @pl.when(core == 0)
    def _():
        place_all((all0, swap1))

    @pl.when(core == 1)
    def _():
        place_all((swap0, all1))


def reduce_prefix(owners, dkp, dvp):
    out = jax.ShapeDtypeStruct((PROMPTS, 64, GROUPS * COLS), jnp.bfloat16)
    spec = pl.BlockSpec(memory_space=VMEM)
    w0, w1 = WIDTHS
    dma = pltpu.SemaphoreType.DMA

    def buf(*shape):
        return VMEM(shape, jnp.bfloat16)

    return pl.pallas_call(
        reduce_kernel,
        out_shape=(out, out),
        in_specs=[pl.BlockSpec(memory_space=pltpu.SMEM), spec, spec],
        out_specs=(spec, spec),
        scratch_shapes=[
            buf(2, PLEN, 768),
            buf(NY, NZ, GROUPS, 16, w0),
            buf(NY, NZ, GROUPS, 16, w1),
            buf(NZ, GROUPS, 16, w0),
            buf(NY, GROUPS, 16, w1),
            buf(NY - 1, NZ, GROUPS, 16, w0),
            buf(NY - 1, GROUPS, 16, w1),
            buf(NZ - 1, GROUPS, 16, w0),
            buf(NZ - 1, NY, GROUPS, 16, w1),
            buf(NY, NZ, GROUPS, 16, w0),
            buf(NY, NZ, GROUPS, 16, w1),
            buf(NY, NZ, GROUPS, 16, w0),
            buf(NY, NZ, GROUPS, 16, w1),
            dma((2,)),
            dma((2,)),
            dma((NY - 1,)),
            dma((NY - 1,)),
            dma((NZ - 1,)),
            dma((NZ - 1,)),
            dma((GROUPS - 1,)),
            dma((GROUPS - 1,)),
            dma((NY - 1,)),
            dma((NY - 1,)),
            dma((NZ - 1,)),
            dma((NZ - 1,)),
            dma((2,)),
            dma((2,)),
        ],
        compiler_params=pltpu.CompilerParams(
            collective_id=2, has_side_effects=True, vmem_limit_bytes=40 << 20
        ),
        name="reduce_prefix",
    )(owners, dkp, dvp)


def per_device(q, k, v, o, g, prefix_k, prefix_v, parents, lengths, prompt_of):
    owners = prompt_of[:, 0]
    pk, pv = gather_prefix(owners, prefix_k, prefix_v)
    dq, dk, dv, dkp, dvp = heads(parents, lengths, q, k, v, o, g, pk, pv)
    prefix_dk, prefix_dv = reduce_prefix(owners, dkp, dvp)
    return dq, dk, dv, prefix_dk, prefix_dv


def solution(mesh):
    split = P("br", "hd")
    held = P(None, "hd", None)
    return jax.shard_map(
        per_device,
        mesh=mesh,
        in_specs=(split,) * 5 + (held, held, P("br", None), P("br", None), P()),
        out_specs=(split,) * 3 + (held, held),
        check_vma=False,
    )
```

```python
import jax
import jax.numpy as jnp
from jax import lax
from jax.experimental import pallas as pl
from jax.experimental.pallas import tpu as pltpu
from jax.sharding import PartitionSpec as P

HS = 128
TILE = 128
BLOCKS = 4
PLEN = 256
PROMPTS = 2
ROWS = 512
HEADS = 10
COLS = 1280
GROUPS = 4
NY = 4
NZ = 8
BATCHES = HEADS // 2
OWN_ROWS = PLEN // GROUPS
SCALE = HS**-0.5
LOG2E = 1.4426950408889634
MESH = pl.DeviceIdType.MESH
VMEM = pltpu.VMEM
BF16 = jnp.bfloat16
F32 = jnp.float32
LAGS = (2, 8, 14, 17, 23, 28, 30)


def place():
    br = lax.axis_index("br")
    return lax.axis_index("hd"), (br // 2) % NY, br // (2 * NY), br % 2


def device(x, y, z, core):
    return ((z * NY + y) * 2 + core, x)


def remote(src, dst, send, recv, who):
    return pltpu.make_async_remote_copy(
        src_ref=src, dst_ref=dst, send_sem=send, recv_sem=recv, device_id=who, device_id_type=MESH
    )


def dot(a, b):
    return jnp.dot(a, b, preferred_element_type=F32)


def dot_t(a, b):
    return lax.dot_general(a, b, (((1,), (1,)), ((), ())), preferred_element_type=F32)


def cols_of(h):
    return pl.ds(pl.multiple_of(h * HS, HS), HS)


def fill_bias(parents, lengths, bias):
    key = lax.broadcasted_iota(jnp.int32, (TILE, TILE), 0)
    query = lax.broadcasted_iota(jnp.int32, (TILE, TILE), 1)
    reach = {}
    for b in range(BLOCKS):
        up = parents[0, b]
        for c in range(b):
            hit = (up == c).astype(jnp.int32)
            for mid in range(c + 1, b):
                hit = hit | ((up == mid).astype(jnp.int32) & reach[mid, c])
            reach[b, c] = hit
    for c in range(BLOCKS):
        for b in range(BLOCKS):
            if b > c:
                seen = key < reach[b, c] * lengths[0, c]
            elif b == c:
                seen = (key < lengths[0, c]) & (key <= query)
            else:
                seen = key < 0
            bias[c * TILE : (c + 1) * TILE, b * TILE : (b + 1) * TILE] = jnp.where(seen, 0.0, -1e30)


def kernel(
    parents, lengths, owner, q_hbm, k_hbm, v_hbm, o_hbm, g_hbm, pk_hbm, pv_hbm,
    dq, dk, dv, out_k, out_v,
    q, k, v, o, g, table_k, table_v, held, pre, bias, e_tree, g_tree, stats, ds_pre,
    part, got1, line, got2, fin, full,
    load_sem, pre_send, pre_recv, s1_send, s1_recv, s2_send, s2_recv, s3_send, s3_recv,
    s4_send, s4_recv, s5_send, s5_recv, s6_send, s6_recv,
):
    x, y, z, core = place()
    mate = device(x, y, z, 1 - core)
    br = lax.axis_index("br")

    barrier = pltpu.get_barrier_semaphore()
    partners = [mate]
    partners += [device((x + d) % GROUPS, y, z, core) for d in range(1, GROUPS)]
    partners += [device(x, (y + d) % NY, z, c) for d in range(1, NY) for c in range(2)]
    partners += [device(x, y, (z + d) % NZ, core) for d in range(1, NZ)]
    for who in partners:
        pl.semaphore_signal(barrier, inc=1, device_id=who, device_id_type=MESH)

    loads = []
    pairs = ((pk_hbm, table_k), (pv_hbm, table_v), (q_hbm, q), (k_hbm, k), (g_hbm, g), (o_hbm, o), (v_hbm, v))
    for i, (src, dst) in enumerate(pairs):
        loads.append(pltpu.make_async_copy(src, dst, load_sem.at[i]))
        loads[-1].start()

    mine = owner[br]
    fill_bias(parents, lengths, bias)
    for a, table in enumerate((table_k, table_v)):
        loads[a].wait()
        for to in range(GROUPS):
            held[a, to] = table[mine, :, to * COLS : (to + 1) * COLS]
    pl.semaphore_wait(barrier, len(partners))

    own_rows = pl.ds(pl.multiple_of(x * OWN_ROWS, OWN_ROWS), OWN_ROWS)
    gathers = []
    for a in range(2):
        for d in range(1, GROUPS):
            gathers.append(
                remote(
                    held.at[a, (x + d) % GROUPS], pre.at[a, own_rows], pre_send.at[a, d - 1], pre_recv.at[a, d - 1],
                    device((x + d) % GROUPS, y, z, core),
                )
            )
            gathers[-1].start()
    for a in range(2):
        pre[a, own_rows] = held[a, x]
    for load in loads[2:]:
        load.wait()

    row = lax.broadcasted_iota(jnp.int32, (TILE, HS), 0)

    @pl.loop(0, HEADS)
    def _(h):
        cols = cols_of(h)
        for pair in range(2):
            rows = pl.ds(256 * pair, 256)
            known = 256 * (pair + 1)
            base = 256 * pair
            qp = q[rows, cols]
            for b in (2 * pair, 2 * pair + 1):
                at = pl.ds(b * TILE, TILE)
                g[at, cols] = jnp.where(row < lengths[0, b], g[at, cols], jnp.zeros((), BF16))
            gp = g[rows, cols]
            row_dot = jnp.sum((gp.astype(F32) * o[rows, cols].astype(F32)).T, axis=0, keepdims=True)
            s = dot_t(k[:known, cols], qp) * (SCALE * LOG2E) + bias[:known, rows]
            top = jnp.max(s, axis=0, keepdims=True)
            e = jnp.exp2(s - top)
            stats[h, pair, 0:1] = top
            stats[h, pair, 1:2] = jnp.sum(e, axis=0, keepdims=True)
            stats[h, pair, 2:3] = row_dot
            e_tree[h, base : base + known] = e
            g_tree[h, base : base + known] = e * (dot_t(v[:known, cols], gp) - row_dot)

    for copy in gathers:
        copy.wait()

    def prompt_part(h):
        cols = cols_of(h)
        key_sum = value_sum = None
        for pair in range(2):
            rows = pl.ds(256 * pair, 256)
            qp, gp = q[rows, cols], g[rows, cols]
            top_tree, sum_tree, row_dot = stats[h, pair, 0:1], stats[h, pair, 1:2], stats[h, pair, 2:3]
            s = dot_t(pre[0, :, cols], qp) * (SCALE * LOG2E)
            top = jnp.maximum(jnp.max(s, axis=0, keepdims=True), top_tree)
            e = jnp.exp2(s - top)
            carry = jnp.exp2(top_tree - top)
            share = 1.0 / (jnp.sum(e, axis=0, keepdims=True) + sum_tree * carry)
            stats[h, pair, 3:4] = carry * share
            att = e * share
            ds = (att * (dot_t(pre[1, :, cols], gp) - row_dot)).astype(BF16)
            ds_pre[h, pair] = ds
            got_k, got_v = dot(ds, qp), dot(att.astype(BF16), gp)
            key_sum = got_k if pair == 0 else key_sum + got_k
            value_sum = got_v if pair == 0 else value_sum + got_v
        j, hp = h // 2, h % 2
        part[j, 2 * hp] = (key_sum * SCALE).astype(BF16)
        part[j, 2 * hp + 1] = value_sum.astype(BF16)

    def tree_part(h):
        cols = cols_of(h)
        keys, pre_keys = k[:, cols].T, pre[0, :, cols].T
        first_k = first_v = None
        for pair in range(2):
            rows = pl.ds(256 * pair, 256)
            known = 256 * (pair + 1)
            base = 256 * pair
            qp, gp = q[rows, cols], g[rows, cols]
            factor = stats[h, pair, 3:4]
            att = (e_tree[h, base : base + known] * factor).astype(BF16)
            ds = (g_tree[h, base : base + known] * factor).astype(BF16)
            got_k, got_v = dot(ds, qp), dot(att, gp)
            dq_t = dot(pre_keys, ds_pre[h, pair]) + dot(keys[:, :known], ds)
            dq[rows, cols] = (dq_t.T * SCALE).astype(BF16)
            if pair == 0:
                first_k, first_v = got_k, got_v
            else:
                dk[:256, cols] = ((first_k + got_k[:256]) * SCALE).astype(BF16)
                dv[:256, cols] = (first_v + got_v[:256]).astype(BF16)
                dk[256:, cols] = (got_k[256:] * SCALE).astype(BF16)
                dv[256:, cols] = got_v[256:].astype(BF16)

    def far1(j, d):
        to = (y + d) % NY
        own = j % 2
        off = (core + own) % 2
        return remote(
            part.at[j, to], got1.at[j, 2 * d + off], s1_send.at[j, d], s1_recv.at[j, 2 * d + off], device(x, to, z, own)
        )

    def land1(j, slot):
        return remote(part.at[j, 0], got1.at[j, slot], s1_send.at[j, 0], s1_recv.at[j, slot], mate)

    def far2(j, d):
        to = (z + d) % NZ
        return remote(line.at[j, to], got2.at[j, d - 1], s2_send.at[j, d - 1], s2_recv.at[j, d - 1], device(x, y, to, core))

    def far3(j, d):
        to = (x + d) % GROUPS
        return remote(
            fin.at[j, to], full.at[j, y, z, x], s3_send.at[j, d - 1], s3_recv.at[j, d - 1], device(to, y, z, core)
        )

    def far4(j, d):
        ref = full.at[j, y, z]
        return remote(ref, ref, s4_send.at[j, d - 1], s4_recv.at[j, d - 1], device(x, y, (z + d) % NZ, core))

    def far5(j, d):
        ref = full.at[j, y]
        return remote(ref, ref, s5_send.at[j, d - 1], s5_recv.at[j, d - 1], device(x, (y + d) % NY, z, core))

    def far6(j, d):
        ref = full.at[j, (y + NY - d) % NY]
        return remote(ref, ref, s6_send.at[j, d], s6_recv.at[j, d], mate)

    def send1(j):
        for d in (2, 1, 3):
            far1(j, d).start()

        @pl.when(core == j % 2)
        def _():
            got1[j, 0] = part[j, y]

        @pl.when(core != j % 2)
        def _():
            far1(j, 0).start()

    def sum1(j):
        for slot in range(1, 2 * NY):
            land1(j, slot).wait_recv()
        weights = []
        for slot in range(2 * NY):
            d, off = slot // 2, slot % 2
            whose = owner[(z * NY + (y + NY - d) % NY) * 2 + (core + off) % 2]
            weights.append([(whose == p).astype(F32) for p in range(PROMPTS)])

        @pl.loop(0, 16)
        def _(tile):
            to, rt = tile // 4, tile % 4
            rows = pl.ds(pl.multiple_of(tile * 16, 16), 16)
            sums = [None] * PROMPTS
            for slot in range(2 * NY):
                term = got1[j, slot, rows].astype(F32)
                for p in range(PROMPTS):
                    scaled = weights[slot][p] * term
                    sums[p] = scaled if slot == 0 else sums[p] + scaled
            for p in range(PROMPTS):
                line[j, 4 * p + rt, to] = sums[p].astype(BF16)

        for d in (4, 3, 5, 2, 6, 1, 7):
            far2(j, d).start()

    def sum2(j):
        for d in range(1, NZ):
            far2(j, d).wait()
        for to in range(GROUPS):
            total = line[j, z, to].astype(F32)
            for d in range(1, NZ):
                total += got2[j, d - 1, to].astype(F32)
            fin[j, to] = total.astype(BF16)
        for d in (2, 1, 3):
            far3(j, d).start()
        full[j, y, z, x] = fin[j, x]

    def share3(j):
        for d in range(1, GROUPS):
            far3(j, d).wait()
        for d in (4, 3, 5, 2, 6, 1, 7):
            far4(j, d).start()

    def share4(j):
        for d in range(1, NZ):
            far4(j, d).wait()
        for d in (2, 1, 3):
            far5(j, d).start()
        far6(j, 0).start()

    def share5(j):
        for d in range(1, NY):
            far5(j, d).wait()
            far6(j, d).start()

    def finish(j):
        @pl.when(core != j % 2)
        def _():
            for d in range(NY):
                far6(j, d).wait_recv()

        @pl.loop(0, NZ)
        def _(t):
            p, rt = t // 4, t % 4
            rows = pl.ds(pl.multiple_of(rt * 16, 16), 16)
            for hp in range(2):
                for a, out in enumerate((out_k, out_v)):
                    for xx in range(GROUPS):
                        at = pl.ds(pl.multiple_of((xx * HEADS + 2 * j + hp) * HS, HS), HS)
                        out[p, rows, at] = full[j, 2 * hp + a, t, xx]

    def stage(step, lag, whole, work):
        j = (step - lag) // 2
        due = (step >= lag) & (step < lag + 2 * BATCHES) & ((step - lag) % 2 == 0)
        if not whole:
            due = due & (core == j % 2)

        @pl.when(due)
        def _():
            work(j)

    @pl.loop(0, 2 * BATCHES + LAGS[-1])
    def _(step):
        @pl.when(step < HEADS)
        def _():
            prompt_part(step)

        @pl.when((step >= HEADS) & (step < 2 * HEADS))
        def _():
            tree_part(step - HEADS)

        stage(step + 1, LAGS[0], True, send1)
        stage(step, LAGS[1], False, sum1)
        stage(step, LAGS[2], False, sum2)
        stage(step, LAGS[3], False, share3)
        stage(step, LAGS[4], False, share4)
        stage(step, LAGS[5], False, share5)
        stage(step, LAGS[6], True, finish)

    @pl.loop(0, BATCHES)
    def _(j):
        for d in range(1, NY):
            far1(j, d).wait_send()

        @pl.when(core != j % 2)
        def _():
            far1(j, 0).wait_send()

        @pl.when(core == j % 2)
        def _():
            for d in range(NY):
                far6(j, d).wait_send()


def fused(parents, lengths, owners, q, k, v, o, g, prefix_k, prefix_v):
    smem = pl.BlockSpec(memory_space=pltpu.SMEM)
    hbm = pl.BlockSpec(memory_space=pltpu.HBM)
    vmem = pl.BlockSpec(memory_space=VMEM)
    big = jax.ShapeDtypeStruct((ROWS, COLS), BF16)
    small = jax.ShapeDtypeStruct((PROMPTS, OWN_ROWS, GROUPS * COLS), BF16)
    sem = pltpu.SemaphoreType.DMA

    def pair(*shape):
        return [sem(shape), sem(shape)]

    return pl.pallas_call(
        kernel,
        out_shape=(big, big, big, small, small),
        in_specs=[smem] * 3 + [hbm] * 7,
        out_specs=(vmem,) * 5,
        scratch_shapes=[VMEM((ROWS, COLS), BF16)] * 5
        + [VMEM((PROMPTS, OWN_ROWS, GROUPS * COLS), BF16)] * 2
        + [
            VMEM((2, GROUPS, OWN_ROWS, COLS), BF16),
            VMEM((2, PLEN, COLS), BF16),
            VMEM((ROWS, ROWS), F32),
            VMEM((HEADS, 768, 256), F32),
            VMEM((HEADS, 768, 256), F32),
            VMEM((HEADS, 2, 8, 256), F32),
            VMEM((HEADS, 2, PLEN, 256), BF16),
            VMEM((BATCHES, NY, PLEN, HS), BF16),
            VMEM((BATCHES, 2 * NY, PLEN, HS), BF16),
            VMEM((BATCHES, NZ, GROUPS, 16, HS), BF16),
            VMEM((BATCHES, NZ - 1, GROUPS, 16, HS), BF16),
            VMEM((BATCHES, GROUPS, 16, HS), BF16),
            VMEM((BATCHES, NY, NZ, GROUPS, 16, HS), BF16),
            sem((7,)),
        ]
        + pair(2, GROUPS - 1)
        + [sem((BATCHES, NY)), sem((BATCHES, 2 * NY))]
        + pair(BATCHES, NZ - 1)
        + pair(BATCHES, GROUPS - 1)
        + pair(BATCHES, NZ - 1)
        + pair(BATCHES, NY - 1)
        + pair(BATCHES, NY),
        compiler_params=pltpu.CompilerParams(
            collective_id=1, has_side_effects=True, vmem_limit_bytes=44 << 20
        ),
        name="tree_grads",
    )(parents, lengths, owners, q, k, v, o, g, prefix_k, prefix_v)


def per_device(q, k, v, o, g, prefix_k, prefix_v, parents, lengths, prompt_of):
    return fused(parents, lengths, prompt_of[:, 0], q, k, v, o, g, prefix_k, prefix_v)


def solution(mesh):
    split = P("br", "hd")
    held = P(None, "hd", None)
    return jax.shard_map(
        per_device,
        mesh=mesh,
        in_specs=(split,) * 5 + (held, held, P("br", None), P("br", None), P()),
        out_specs=(split,) * 3 + (held, held),
        check_vma=False,
    )
```

```python
import jax
import jax.numpy as jnp
from jax import lax
from jax.experimental import pallas as pl
from jax.experimental.pallas import tpu as pltpu
from jax.sharding import PartitionSpec as P

HS = 128
TILE = 128
BLOCKS = 4
PLEN = 256
PROMPTS = 2
ROWS = 512
HEADS = 10
COLS = 1280
GROUPS = 4
NY = 4
NZ = 8
BATCHES = HEADS // 2
OWN_ROWS = PLEN // GROUPS
SCALE = HS**-0.5
LOG2E = 1.4426950408889634
MESH = pl.DeviceIdType.MESH
VMEM = pltpu.VMEM
BF16 = jnp.bfloat16
F32 = jnp.float32
LAGS = (4, 14, 26, 36, 45, 62)
VMEM_BYTES = 47 << 20
AT_PARENTS = 64
AT_LENGTHS = 68
WORDS = 72


def place():
    br = lax.axis_index("br")
    return lax.axis_index("hd"), (br // 2) % NY, br // (2 * NY), br % 2


def device(x, y, z, core):
    return ((z * NY + y) * 2 + core, x)


def remote(src, dst, send, recv, who):
    return pltpu.make_async_remote_copy(
        src_ref=src, dst_ref=dst, send_sem=send, recv_sem=recv, device_id=who, device_id_type=MESH
    )


def dot(a, b):
    return jnp.dot(a, b, preferred_element_type=F32)


def dot_t(a, b):
    return lax.dot_general(a, b, (((1,), (1,)), ((), ())), preferred_element_type=F32)


def cols_of(h):
    return pl.ds(pl.multiple_of(h * HS, HS), HS)


def fill_bias(words, bias):
    key = lax.broadcasted_iota(jnp.int32, (TILE, TILE), 0)
    query = lax.broadcasted_iota(jnp.int32, (TILE, TILE), 1)
    reach = {}
    for b in range(BLOCKS):
        up = words[AT_PARENTS + b]
        for c in range(b):
            hit = (up == c).astype(jnp.int32)
            for mid in range(c + 1, b):
                hit = hit | ((up == mid).astype(jnp.int32) & reach[mid, c])
            reach[b, c] = hit
    for c in range(BLOCKS):
        for b in range(BLOCKS):
            if b > c:
                seen = key < reach[b, c] * words[AT_LENGTHS + c]
            elif b == c:
                seen = (key < words[AT_LENGTHS + c]) & (key <= query)
            else:
                seen = key < 0
            bias[c * TILE : (c + 1) * TILE, b * TILE : (b + 1) * TILE] = jnp.where(seen, 0.0, -1e30)


def kernel(
    words_hbm, q_hbm, k_hbm, v_hbm, o_hbm, g_hbm, pk_hbm, pv_hbm,
    dq, dk, dv, sums_k, sums_v,
    words, q, k, v, o, g, t0, t1, t2, t3, t4, t5, t6, t7, held, pre, bias, e_tree, g_tree, att_pre, ds_pre, stats,
    part, got1, line, got2,
    word_sem, table_sem, load_sem, pre_send, pre_recv, s1_send, s1_recv, s2_send, s2_recv,
    s4_send, s4_recv, s5_send, s5_recv, s6_send, s6_recv,
):
    x, y, z, core = place()
    mate = device(x, y, z, 1 - core)
    br = lax.axis_index("br")

    barrier = pltpu.get_barrier_semaphore()
    partners = [device(x, y, (z + d) % NZ, core) for d in (4, 3, 5, 2, 6)]
    partners += [
        device((x + dx) % GROUPS, (y + dy) % NY, z, c)
        for dx in (2, 1, 3, 0)
        for dy in (2, 1, 3, 0)
        for c in ((core, 1 - core) if dx or dy else (1 - core,))
    ]
    partners += [device(x, y, (z + d) % NZ, core) for d in (1, 7)]
    for who in partners:
        pl.semaphore_signal(barrier, inc=1, device_id=who, device_id_type=MESH)

    get_words = pltpu.make_async_copy(words_hbm, words, word_sem)
    get_words.start()
    table = ((t0, t1, t2, t3), (t4, t5, t6, t7))
    order = [(x + d) % GROUPS for d in (2, 1, 3, 0)]
    tables = []
    for a, src in enumerate((pk_hbm, pv_hbm)):
        for i, to in enumerate(order):
            at = pl.ds(pl.multiple_of(to * COLS, COLS), COLS)
            tables.append(pltpu.make_async_copy(src.at[:, :, at], table[a][i], table_sem.at[a, i]))
            tables[-1].start()
    get_words.wait()
    mine = words[br]

    def gather(a, i):
        d = (2, 1, 3)[i]
        return remote(
            held.at[a, i], pre.at[a, own_rows], pre_send.at[a, i], pre_recv.at[a, i],
            device((x + d) % GROUPS, y, z, core),
        )

    own_rows = pl.ds(pl.multiple_of(x * OWN_ROWS, OWN_ROWS), OWN_ROWS)
    pl.semaphore_wait(barrier, len(partners))
    loads = []
    for a in range(2):
        for i in range(GROUPS):
            tables[GROUPS * a + i].wait()
            if i < 3:
                held[a, i] = table[a][i][mine]
                gather(a, i).start()
            else:
                pre[a, own_rows] = table[a][i][mine]
        if a == 0:
            for i, (src, dst) in enumerate(((q_hbm, q), (k_hbm, k), (g_hbm, g), (o_hbm, o), (v_hbm, v))):
                loads.append(pltpu.make_async_copy(src, dst, load_sem.at[i]))
                loads[-1].start()
    fill_bias(words, bias)
    for load in loads:
        load.wait()

    row = lax.broadcasted_iota(jnp.int32, (TILE, HS), 0)

    @pl.loop(0, HEADS)
    def _(h):
        cols = cols_of(h)
        for pair in range(2):
            rows = pl.ds(256 * pair, 256)
            known = 256 * (pair + 1)
            base = 256 * pair
            qp = q[rows, cols]
            for b in (2 * pair, 2 * pair + 1):
                at = pl.ds(b * TILE, TILE)
                g[at, cols] = jnp.where(row < words[AT_LENGTHS + b], g[at, cols], jnp.zeros((), BF16))
            gp = g[rows, cols]
            row_dot = jnp.sum((gp.astype(F32) * o[rows, cols].astype(F32)).T, axis=0, keepdims=True)
            s = dot_t(k[:known, cols], qp) * (SCALE * LOG2E) + bias[:known, rows]
            top = jnp.max(s, axis=0, keepdims=True)
            e = jnp.exp2(s - top)
            stats[h, pair, 0:1] = top
            stats[h, pair, 1:2] = jnp.sum(e, axis=0, keepdims=True)
            stats[h, pair, 2:3] = row_dot
            e_tree[h, base : base + known] = e
            g_tree[h, base : base + known] = e * (dot_t(v[:known, cols], gp) - row_dot)

    for i in range(3):
        gather(0, i).wait()

    def value_part(h):
        cols = cols_of(h)
        value_sum = None
        for pair in range(2):
            rows = pl.ds(256 * pair, 256)
            top_tree, sum_tree = stats[h, pair, 0:1], stats[h, pair, 1:2]
            s = dot_t(pre[0, :, cols], q[rows, cols]) * (SCALE * LOG2E)
            top = jnp.maximum(jnp.max(s, axis=0, keepdims=True), top_tree)
            e = jnp.exp2(s - top)
            carry = jnp.exp2(top_tree - top)
            share = 1.0 / (jnp.sum(e, axis=0, keepdims=True) + sum_tree * carry)
            stats[h, pair, 3:4] = carry * share
            att = e * share
            att_pre[h, pair] = att
            got = dot(att.astype(BF16), g[rows, cols])
            value_sum = got if pair == 0 else value_sum + got
        part[h // 4, h % 4] = value_sum.astype(BF16)

    def key_part(i):
        h, u = (i + 8) % HEADS, i + HEADS
        cols = cols_of(h)
        key_sum = None
        for pair in range(2):
            rows = pl.ds(256 * pair, 256)
            row_dot = stats[h, pair, 2:3]
            ds = (att_pre[h, pair] * (dot_t(pre[1, :, cols], g[rows, cols]) - row_dot)).astype(BF16)
            ds_pre[h, pair] = ds
            got = dot(ds, q[rows, cols])
            key_sum = got if pair == 0 else key_sum + got
        part[u // 4, u % 4] = (key_sum * SCALE).astype(BF16)

    def tree_part(h):
        cols = cols_of(h)
        keys, pre_keys = k[:, cols].T, pre[0, :, cols].T
        first_k = first_v = None
        for pair in range(2):
            rows = pl.ds(256 * pair, 256)
            known = 256 * (pair + 1)
            base = 256 * pair
            qp, gp = q[rows, cols], g[rows, cols]
            factor = stats[h, pair, 3:4]
            att = (e_tree[h, base : base + known] * factor).astype(BF16)
            ds = (g_tree[h, base : base + known] * factor).astype(BF16)
            got_k, got_v = dot(ds, qp), dot(att, gp)
            dq_t = dot(pre_keys, ds_pre[h, pair]) + dot(keys[:, :known], ds)
            dq[rows, cols] = (dq_t.T * SCALE).astype(BF16)
            if pair == 0:
                first_k, first_v = got_k, got_v
            else:
                dk[:256, cols] = ((first_k + got_k[:256]) * SCALE).astype(BF16)
                dv[:256, cols] = (first_v + got_v[:256]).astype(BF16)
                dk[256:, cols] = (got_k[256:] * SCALE).astype(BF16)
                dv[256:, cols] = got_v[256:].astype(BF16)

    def slot_of(dx, dy, off):
        return (dx * NY + dy) * 2 + off

    def sent(ref, sem):
        remote(ref, ref, sem, s1_recv.at[0], mate).wait_send()

    def landed(ref, sem):
        remote(ref, ref, s1_send.at[0], sem, mate).wait_recv()

    def with_unit(j, yy, work):
        u = NY * j + yy
        late = u // HEADS
        cols = cols_of((u - 2 * late) % HEADS)
        for which, ref in enumerate((sums_v, sums_k)):

            @pl.when(late == which)
            def _(ref=ref):
                work(ref, cols)

    def rows_of(zz):
        return zz // 4, pl.ds(pl.multiple_of(zz % 4 * 16, 16), 16)

    def far1(j, dx, dy):
        to_x, to_y = (x + dx) % GROUPS, (y + dy) % NY
        own = j % 2
        rows = pl.ds(pl.multiple_of(to_x * OWN_ROWS, OWN_ROWS), OWN_ROWS)
        return remote(
            part.at[j, to_y, rows], got1.at[j, slot_of(dx, dy, (core + own) % 2)], s1_send.at[j], s1_recv.at[j],
            device(to_x, to_y, z, own),
        )

    def far2(j, d):
        to = (z + d) % NZ
        return remote(line.at[j, to], got2.at[j, d - 1], s2_send.at[j], s2_recv.at[j], device(x, y, to, core))

    def far4(j, d, ref):
        return remote(ref, ref, s4_send.at[j], s4_recv.at[j], device(x, y, (z + d) % NZ, core))

    def far5(j, d, ref):
        return remote(ref, ref, s5_send.at[j], s5_recv.at[j, d - 1], device(x, (y + d) % NY, z, core))

    def far6(j, ref):
        return remote(ref, ref, s6_send.at[j], s6_recv.at[j], mate)

    def send1(j):
        for dy in (2, 1, 3, 0):
            for dx in (2, 1, 3, 0):
                if dx or dy:
                    far1(j, dx, dy).start()

        @pl.when(core == j % 2)
        def _():
            got1[j, 0] = part[j, y, own_rows]

        @pl.when(core != j % 2)
        def _():
            far1(j, 0, 0).start()

    def sum1(j):
        landed(got1.at[j, pl.ds(1, 2 * NY * GROUPS - 1)], s1_recv.at[j])
        weights = []
        for dy in range(NY):
            for off in range(2):
                whose = words[(z * NY + (y + NY - dy) % NY) * 2 + (core + off) % 2]
                weights.append([(whose == p).astype(F32) for p in range(PROMPTS)])

        @pl.loop(0, 16)
        def _(tile):
            dx, rt = tile // 4, tile % 4
            rows = pl.ds(pl.multiple_of(rt * 16, 16), 16)
            sums = [None] * PROMPTS
            for i in range(2 * NY):
                term = got1[j, dx * 2 * NY + i, rows].astype(F32)
                for p in range(PROMPTS):
                    scaled = weights[i][p] * term
                    sums[p] = scaled if i == 0 else sums[p] + scaled
            for p in range(PROMPTS):
                line[j, 4 * p + rt, (x + GROUPS - dx) % GROUPS] = sums[p].astype(BF16)

        for d in (4, 3, 5, 2, 6, 1, 7):
            far2(j, d).start()

    def sum2(j):
        landed(got2.at[j], s2_recv.at[j])
        sent(got2.at[j], s2_send.at[j])
        p, rows = rows_of(z)

        def work(sums, cols):
            for xx in range(GROUPS):
                total = line[j, z, xx].astype(F32)
                for d in range(1, NZ):
                    total += got2[j, d - 1, xx].astype(F32)
                sums[xx, p, rows, cols] = total.astype(BF16)
            for d in (4, 3, 5, 2, 6, 1, 7):
                far4(j, d, sums.at[:, p, rows, cols]).start()

        with_unit(j, y, work)

    def share4(j):
        landed(got2.at[j], s4_recv.at[j])

        def work(sums, cols):
            ref = sums.at[:, :, :, cols]
            for d in (2, 1, 3):
                far5(j, d, ref).start()
            far6(j, ref).start()

        with_unit(j, y, work)

    def share5(j):
        for d in (1, 3, 2):
            landed(got1.at[j, pl.ds(0, 2 * NY)], s5_recv.at[j, d - 1])
            with_unit(j, (y + NY - d) % NY, lambda sums, cols: far6(j, sums.at[:, :, :, cols]).start())

    def finish(j):
        @pl.when(core != j % 2)
        def _():
            landed(got1.at[j], s6_recv.at[j])

    def stage(step, lag, whole, work):
        j = (step - lag) // 4
        due = (step >= lag) & (step < lag + 4 * BATCHES) & ((step - lag) % 4 == 0)
        if not whole:
            due = due & (core == j % 2)

        @pl.when(due)
        def _():
            work(j)

    @pl.loop(0, 4 * BATCHES + LAGS[-1])
    def _(step):
        @pl.when(step < HEADS)
        def _():
            value_part(step)

        @pl.when(step == HEADS)
        def _():
            for i in range(3):
                gather(1, i).wait()

        @pl.when((step >= HEADS) & (step < 2 * HEADS))
        def _():
            key_part(step - HEADS)

        stage(step + 1, LAGS[0], True, send1)

        @pl.when((step >= 2 * HEADS) & (step < 3 * HEADS))
        def _():
            tree_part(step - 2 * HEADS)

        stage(step, LAGS[1], False, sum1)
        stage(step, LAGS[2], False, sum2)
        stage(step, LAGS[3], False, share4)
        stage(step, LAGS[4], False, share5)
        stage(step, LAGS[5], True, finish)

    @pl.loop(0, BATCHES)
    def _(j):
        sent(got1.at[j, pl.ds(0, NY * GROUPS - 1)], s1_send.at[j])

        @pl.when(core != j % 2)
        def _():
            sent(got1.at[j, 0], s1_send.at[j])

        @pl.when(core == j % 2)
        def _():
            sent(got2.at[j], s4_send.at[j])
            sent(got1.at[j, pl.ds(0, 3 * 2 * NY)], s5_send.at[j])
            sent(got1.at[j], s6_send.at[j])


def fused(words, q, k, v, o, g, prefix_k, prefix_v):
    smem = pltpu.SMEM
    hbm = pl.BlockSpec(memory_space=pltpu.HBM)
    vmem = pl.BlockSpec(memory_space=VMEM)
    big = jax.ShapeDtypeStruct((ROWS, COLS), BF16)
    small = jax.ShapeDtypeStruct((GROUPS, PROMPTS, OWN_ROWS, COLS), BF16)
    sem = pltpu.SemaphoreType.DMA

    def pair(*shape):
        return [sem(shape), sem(shape)]

    return pl.pallas_call(
        kernel,
        out_shape=(big, big, big, small, small),
        in_specs=[hbm] * 8,
        out_specs=(vmem,) * 5,
        scratch_shapes=[smem((WORDS,), jnp.int32)]
        + [VMEM((ROWS, COLS), BF16)] * 5
        + [VMEM((PROMPTS, OWN_ROWS, COLS), BF16)] * (2 * GROUPS)
        + [
            VMEM((2, GROUPS - 1, OWN_ROWS, COLS), BF16),
            VMEM((2, PLEN, COLS), BF16),
            VMEM((ROWS, ROWS), F32),
            VMEM((HEADS, 768, 256), F32),
            VMEM((HEADS, 768, 256), F32),
            VMEM((HEADS, 2, PLEN, 256), F32),
            VMEM((HEADS, 2, PLEN, 256), BF16),
            VMEM((HEADS, 2, 8, 256), F32),
            VMEM((BATCHES, NY, PLEN, HS), BF16),
            VMEM((BATCHES, 2 * NY * GROUPS, OWN_ROWS, HS), BF16),
            VMEM((BATCHES, NZ, GROUPS, 16, HS), BF16),
            VMEM((BATCHES, NZ - 1, GROUPS, 16, HS), BF16),
            sem,
            sem((2, GROUPS)),
            sem((5,)),
        ]
        + pair(2, GROUPS - 1)
        + pair(BATCHES)
        + pair(BATCHES)
        + pair(BATCHES)
        + [sem((BATCHES,)), sem((BATCHES, NY - 1))]
        + pair(BATCHES),
        compiler_params=pltpu.CompilerParams(
            collective_id=1, has_side_effects=True, vmem_limit_bytes=VMEM_BYTES
        ),
        name="tree_grads",
    )(words, q, k, v, o, g, prefix_k, prefix_v)


def write_kernel(dq, dk, dv, sums_k, sums_v, dq_out, dk_out, dv_out, key_out, value_out, sems):
    pairs = [(dq, dq_out), (dk, dk_out), (dv, dv_out)]
    for sums, out in ((sums_k, key_out), (sums_v, value_out)):
        pairs += [(sums.at[xx], out.at[:, :, pl.ds(xx * COLS, COLS)]) for xx in range(GROUPS)]
    copies = [pltpu.make_async_copy(src, dst, sems.at[i]) for i, (src, dst) in enumerate(pairs)]
    for copy in copies:
        copy.start()
    for copy in copies:
        copy.wait()


def write(dq, dk, dv, sums_k, sums_v):
    big = jax.ShapeDtypeStruct((ROWS, COLS), BF16)
    small = jax.ShapeDtypeStruct((PROMPTS, OWN_ROWS, GROUPS * COLS), BF16)
    return pl.pallas_call(
        write_kernel,
        out_shape=(big, big, big, small, small),
        in_specs=[pl.BlockSpec(memory_space=VMEM)] * 5,
        out_specs=(pl.BlockSpec(memory_space=pltpu.HBM),) * 5,
        scratch_shapes=[pltpu.SemaphoreType.DMA((3 + 2 * GROUPS,))],
        compiler_params=pltpu.CompilerParams(vmem_limit_bytes=1 << 20),
        name="write",
    )(dq, dk, dv, sums_k, sums_v)


def per_device(q, k, v, o, g, prefix_k, prefix_v, parents, lengths, prompt_of):
    words = jnp.concatenate([prompt_of[:, 0], parents[0], lengths[0]])
    return write(*fused(words, q, k, v, o, g, prefix_k, prefix_v))


def solution(mesh):
    split = P("br", "hd")
    held = P(None, "hd", None)
    return jax.shard_map(
        per_device,
        mesh=mesh,
        in_specs=(split,) * 5 + (held, held, P("br", None), P("br", None), P()),
        out_specs=(split,) * 3 + (held, held),
        check_vma=False,
    )
```

```python
import jax
import jax.numpy as jnp
from jax import lax
from jax.experimental import pallas as pl
from jax.experimental.pallas import tpu as pltpu
from jax.sharding import PartitionSpec as P

HS = 128
TILE = 128
BLOCKS = 4
PLEN = 256
PROMPTS = 2
ROWS = 512
HEADS = 10
COLS = 1280
GROUPS = 4
NY = 4
NZ = 8
BATCHES = HEADS // 2
OWN_ROWS = PLEN // GROUPS
SCALE = HS**-0.5
LOG2E = 1.4426950408889634
MESH = pl.DeviceIdType.MESH
VMEM = pltpu.VMEM
BF16 = jnp.bfloat16
F32 = jnp.float32
LAGS = (4, 11, 20, 28, 36, 52)
VMEM_BYTES = 47 << 20
AT_PARENTS = 64
AT_LENGTHS = 68
WORDS = 72


def place():
    br = lax.axis_index("br")
    return lax.axis_index("hd"), (br // 2) % NY, br // (2 * NY), br % 2


def device(x, y, z, core):
    return ((z * NY + y) * 2 + core, x)


def remote(src, dst, send, recv, who):
    return pltpu.make_async_remote_copy(
        src_ref=src, dst_ref=dst, send_sem=send, recv_sem=recv, device_id=who, device_id_type=MESH
    )


def dot(a, b):
    return jnp.dot(a, b, preferred_element_type=F32)


def dot_t(a, b):
    return lax.dot_general(a, b, (((1,), (1,)), ((), ())), preferred_element_type=F32)


def cols_of(h):
    return pl.ds(pl.multiple_of(h * HS, HS), HS)


def fill_bias(words, bias):
    key = lax.broadcasted_iota(jnp.int32, (TILE, TILE), 0)
    query = lax.broadcasted_iota(jnp.int32, (TILE, TILE), 1)
    reach = {}
    for b in range(BLOCKS):
        up = words[AT_PARENTS + b]
        for c in range(b):
            hit = (up == c).astype(jnp.int32)
            for mid in range(c + 1, b):
                hit = hit | ((up == mid).astype(jnp.int32) & reach[mid, c])
            reach[b, c] = hit
    for c in range(BLOCKS):
        for b in range(BLOCKS):
            if b > c:
                seen = key < reach[b, c] * words[AT_LENGTHS + c]
            elif b == c:
                seen = (key < words[AT_LENGTHS + c]) & (key <= query)
            else:
                seen = key < 0
            bias[c * TILE : (c + 1) * TILE, b * TILE : (b + 1) * TILE] = jnp.where(seen, 0.0, -1e30)


def kernel(
    words_hbm, q_hbm, k_hbm, v_hbm, o_hbm, g_hbm, pk_hbm, pv_hbm,
    dq, dk, dv, sums_k, sums_v,
    words, q, k, v, o, g, t0, t1, t2, t3, t4, t5, t6, t7, held, pre, bias, e_tree, g_tree, att_pre, ds_pre, stats,
    part, got1, line, got2,
    word_sem, table_sem, load_sem, pre_send, pre_recv, s1_send, s1_recv, s2_send, s2_recv,
    s4_send, s4_recv, s5_send, s5_recv, s6_send, s6_recv,
):
    x, y, z, core = place()
    mate = device(x, y, z, 1 - core)
    br = lax.axis_index("br")

    barrier = pltpu.get_barrier_semaphore()
    partners = [device(x, y, (z + d) % NZ, core) for d in (4, 3, 5, 2, 6)]
    partners += [
        device((x + dx) % GROUPS, (y + dy) % NY, z, c)
        for dx in (2, 1, 3, 0)
        for dy in (2, 1, 3, 0)
        for c in ((core, 1 - core) if dx or dy else (1 - core,))
    ]
    partners += [device(x, y, (z + d) % NZ, core) for d in (1, 7)]
    for who in partners:
        pl.semaphore_signal(barrier, inc=1, device_id=who, device_id_type=MESH)

    get_words = pltpu.make_async_copy(words_hbm, words, word_sem)
    get_words.start()
    table = ((t0, t1, t2, t3), (t4, t5, t6, t7))
    order = [(x + d) % GROUPS for d in (2, 1, 3, 0)]
    tables = []
    for a, src in enumerate((pk_hbm, pv_hbm)):
        for i, to in enumerate(order):
            at = pl.ds(pl.multiple_of(to * COLS, COLS), COLS)
            tables.append(pltpu.make_async_copy(src.at[:, :, at], table[a][i], table_sem.at[a, i]))
            tables[-1].start()
    get_words.wait()
    mine = words[br]

    def gather(a, i):
        d = (2, 1, 3)[i]
        return remote(
            held.at[a, i], pre.at[a, own_rows], pre_send.at[a, i], pre_recv.at[a, i],
            device((x + d) % GROUPS, y, z, core),
        )

    own_rows = pl.ds(pl.multiple_of(x * OWN_ROWS, OWN_ROWS), OWN_ROWS)
    pl.semaphore_wait(barrier, len(partners))
    loads = []
    for a in range(2):
        for i in range(GROUPS):
            tables[GROUPS * a + i].wait()
            if i < 3:
                held[a, i] = table[a][i][mine]
                gather(a, i).start()
            else:
                pre[a, own_rows] = table[a][i][mine]
        if a == 0:
            for i, (src, dst) in enumerate(((q_hbm, q), (k_hbm, k), (g_hbm, g), (o_hbm, o), (v_hbm, v))):
                loads.append(pltpu.make_async_copy(src, dst, load_sem.at[i]))
                loads[-1].start()
    fill_bias(words, bias)
    for load in loads:
        load.wait()

    row = lax.broadcasted_iota(jnp.int32, (TILE, HS), 0)

    @pl.loop(0, HEADS)
    def _(h):
        cols = cols_of(h)
        for pair in range(2):
            rows = pl.ds(256 * pair, 256)
            known = 256 * (pair + 1)
            base = 256 * pair
            qp = q[rows, cols]
            for b in (2 * pair, 2 * pair + 1):
                at = pl.ds(b * TILE, TILE)
                g[at, cols] = jnp.where(row < words[AT_LENGTHS + b], g[at, cols], jnp.zeros((), BF16))
            gp = g[rows, cols]
            row_dot = jnp.sum((gp.astype(F32) * o[rows, cols].astype(F32)).T, axis=0, keepdims=True)
            s = dot_t(k[:known, cols], qp) * (SCALE * LOG2E) + bias[:known, rows]
            top = jnp.max(s, axis=0, keepdims=True)
            e = jnp.exp2(s - top)
            stats[h, pair, 0:1] = top
            stats[h, pair, 1:2] = jnp.sum(e, axis=0, keepdims=True)
            stats[h, pair, 2:3] = row_dot
            e_tree[h, base : base + known] = e
            g_tree[h, base : base + known] = e * (dot_t(v[:known, cols], gp) - row_dot)

    for i in range(3):
        gather(0, i).wait()

    def value_part(h):
        cols = cols_of(h)
        value_sum = None
        for pair in range(2):
            rows = pl.ds(256 * pair, 256)
            top_tree, sum_tree = stats[h, pair, 0:1], stats[h, pair, 1:2]
            s = dot_t(pre[0, :, cols], q[rows, cols]) * (SCALE * LOG2E)
            top = jnp.maximum(jnp.max(s, axis=0, keepdims=True), top_tree)
            e = jnp.exp2(s - top)
            carry = jnp.exp2(top_tree - top)
            share = 1.0 / (jnp.sum(e, axis=0, keepdims=True) + sum_tree * carry)
            stats[h, pair, 3:4] = carry * share
            att = e * share
            att_pre[h, pair] = att
            got = dot(att.astype(BF16), g[rows, cols])
            value_sum = got if pair == 0 else value_sum + got
        part[h // 4, h % 4] = value_sum.astype(BF16)

    def key_part(i):
        h, u = (i + 8) % HEADS, i + HEADS
        cols = cols_of(h)
        key_sum = None
        for pair in range(2):
            rows = pl.ds(256 * pair, 256)
            row_dot = stats[h, pair, 2:3]
            ds = (att_pre[h, pair] * (dot_t(pre[1, :, cols], g[rows, cols]) - row_dot)).astype(BF16)
            ds_pre[h, pair] = ds
            got = dot(ds, q[rows, cols])
            key_sum = got if pair == 0 else key_sum + got
        part[u // 4, u % 4] = (key_sum * SCALE).astype(BF16)

    def tree_part(h):
        cols = cols_of(h)
        keys, pre_keys = k[:, cols].T, pre[0, :, cols].T
        first_k = first_v = None
        for pair in range(2):
            rows = pl.ds(256 * pair, 256)
            known = 256 * (pair + 1)
            base = 256 * pair
            qp, gp = q[rows, cols], g[rows, cols]
            factor = stats[h, pair, 3:4]
            att = (e_tree[h, base : base + known] * factor).astype(BF16)
            ds = (g_tree[h, base : base + known] * factor).astype(BF16)
            got_k, got_v = dot(ds, qp), dot(att, gp)
            dq_t = dot(pre_keys, ds_pre[h, pair]) + dot(keys[:, :known], ds)
            dq[rows, cols] = (dq_t.T * SCALE).astype(BF16)
            if pair == 0:
                first_k, first_v = got_k, got_v
            else:
                dk[:256, cols] = ((first_k + got_k[:256]) * SCALE).astype(BF16)
                dv[:256, cols] = (first_v + got_v[:256]).astype(BF16)
                dk[256:, cols] = (got_k[256:] * SCALE).astype(BF16)
                dv[256:, cols] = got_v[256:].astype(BF16)

    def slot_of(dx, dy, off):
        return (dx * NY + dy) * 2 + off

    def sent(ref, sem):
        remote(ref, ref, sem, s1_recv.at[0], mate).wait_send()

    def landed(ref, sem):
        remote(ref, ref, s1_send.at[0], sem, mate).wait_recv()

    def with_unit(j, yy, work):
        u = NY * j + yy
        late = u // HEADS
        cols = cols_of((u - 2 * late) % HEADS)
        for which, ref in enumerate((sums_v, sums_k)):

            @pl.when(late == which)
            def _(ref=ref):
                work(ref, cols)

    def rows_of(zz):
        return zz // 4, pl.ds(pl.multiple_of(zz % 4 * 16, 16), 16)

    def far1(j, dx, dy):
        to_x, to_y = (x + dx) % GROUPS, (y + dy) % NY
        own = j % 2
        rows = pl.ds(pl.multiple_of(to_x * OWN_ROWS, OWN_ROWS), OWN_ROWS)
        return remote(
            part.at[j, to_y, rows], got1.at[j, slot_of(dx, dy, (core + own) % 2)], s1_send.at[j], s1_recv.at[j],
            device(to_x, to_y, z, own),
        )

    def far2(j, d):
        to = (z + d) % NZ
        return remote(line.at[j, to], got2.at[j, d - 1], s2_send.at[j], s2_recv.at[j], device(x, y, to, core))

    def far4(j, d, ref):
        return remote(ref, ref, s4_send.at[j], s4_recv.at[j], device(x, y, (z + d) % NZ, core))

    def far5(j, d, ref):
        return remote(ref, ref, s5_send.at[j], s5_recv.at[j, d - 1], device(x, (y + d) % NY, z, core))

    def far6(j, ref):
        return remote(ref, ref, s6_send.at[j], s6_recv.at[j], mate)

    def send1(j):
        for dy in (2, 1, 3, 0):
            for dx in (2, 1, 3, 0):
                if dx or dy:
                    far1(j, dx, dy).start()

        @pl.when(core == j % 2)
        def _():
            got1[j, 0] = part[j, y, own_rows]

        @pl.when(core != j % 2)
        def _():
            far1(j, 0, 0).start()

    def sum1(j):
        landed(got1.at[j, pl.ds(1, 2 * NY * GROUPS - 1)], s1_recv.at[j])
        weights = []
        for dy in range(NY):
            for off in range(2):
                whose = words[(z * NY + (y + NY - dy) % NY) * 2 + (core + off) % 2]
                weights.append([(whose == p).astype(F32) for p in range(PROMPTS)])

        @pl.loop(0, 16)
        def _(tile):
            dx, rt = tile // 4, tile % 4
            rows = pl.ds(pl.multiple_of(rt * 16, 16), 16)
            sums = [None] * PROMPTS
            for i in range(2 * NY):
                term = got1[j, dx * 2 * NY + i, rows].astype(F32)
                for p in range(PROMPTS):
                    scaled = weights[i][p] * term
                    sums[p] = scaled if i == 0 else sums[p] + scaled
            for p in range(PROMPTS):
                line[j, 4 * p + rt, (x + GROUPS - dx) % GROUPS] = sums[p].astype(BF16)

        for d in (4, 3, 5, 2, 6, 1, 7):
            far2(j, d).start()

    def sum2(j):
        landed(got2.at[j], s2_recv.at[j])
        sent(got2.at[j], s2_send.at[j])
        p, rows = rows_of(z)

        def work(sums, cols):
            for xx in range(GROUPS):
                total = line[j, z, xx].astype(F32)
                for d in range(1, NZ):
                    total += got2[j, d - 1, xx].astype(F32)
                sums[xx, p, rows, cols] = total.astype(BF16)
            for d in (4, 3, 5, 2, 6, 1, 7):
                far4(j, d, sums.at[:, p, rows, cols]).start()

        with_unit(j, y, work)

    def share4(j):
        landed(got2.at[j], s4_recv.at[j])

        def work(sums, cols):
            ref = sums.at[:, :, :, cols]
            for d in (2, 1, 3):
                far5(j, d, ref).start()
            far6(j, ref).start()

        with_unit(j, y, work)

    def share5(j):
        for d in (1, 3, 2):
            landed(got1.at[j, pl.ds(0, 2 * NY)], s5_recv.at[j, d - 1])
            with_unit(j, (y + NY - d) % NY, lambda sums, cols: far6(j, sums.at[:, :, :, cols]).start())

    def finish(j):
        @pl.when(core != j % 2)
        def _():
            landed(got1.at[j], s6_recv.at[j])

    def stage(step, lag, whole, work):
        j = (step - lag) // 4
        due = (step >= lag) & (step < lag + 4 * BATCHES) & ((step - lag) % 4 == 0)
        if not whole:
            due = due & (core == j % 2)

        @pl.when(due)
        def _():
            work(j)

    @pl.loop(0, 4 * BATCHES + LAGS[-1])
    def _(step):
        @pl.when(step < HEADS)
        def _():
            value_part(step)

        @pl.when(step == HEADS)
        def _():
            for i in range(3):
                gather(1, i).wait()

        @pl.when((step >= HEADS) & (step < 2 * HEADS))
        def _():
            key_part(step - HEADS)

        stage(step + 1, LAGS[0], True, send1)

        @pl.when((step >= 2 * HEADS) & (step < 3 * HEADS))
        def _():
            tree_part(step - 2 * HEADS)

        stage(step, LAGS[1], False, sum1)
        stage(step, LAGS[2], False, sum2)
        stage(step, LAGS[3], False, share4)
        stage(step, LAGS[4], False, share5)
        stage(step, LAGS[5], True, finish)

    @pl.loop(0, BATCHES)
    def _(j):
        sent(got1.at[j, pl.ds(0, NY * GROUPS - 1)], s1_send.at[j])

        @pl.when(core != j % 2)
        def _():
            sent(got1.at[j, 0], s1_send.at[j])

        @pl.when(core == j % 2)
        def _():
            sent(got2.at[j], s4_send.at[j])
            sent(got1.at[j, pl.ds(0, 3 * 2 * NY)], s5_send.at[j])
            sent(got1.at[j], s6_send.at[j])


def fused(words, q, k, v, o, g, prefix_k, prefix_v):
    smem = pltpu.SMEM
    hbm = pl.BlockSpec(memory_space=pltpu.HBM)
    vmem = pl.BlockSpec(memory_space=VMEM)
    big = jax.ShapeDtypeStruct((ROWS, COLS), BF16)
    small = jax.ShapeDtypeStruct((GROUPS, PROMPTS, OWN_ROWS, COLS), BF16)
    sem = pltpu.SemaphoreType.DMA

    def pair(*shape):
        return [sem(shape), sem(shape)]

    return pl.pallas_call(
        kernel,
        out_shape=(big, big, big, small, small),
        in_specs=[hbm] * 8,
        out_specs=(vmem,) * 5,
        scratch_shapes=[smem((WORDS,), jnp.int32)]
        + [VMEM((ROWS, COLS), BF16)] * 5
        + [VMEM((PROMPTS, OWN_ROWS, COLS), BF16)] * (2 * GROUPS)
        + [
            VMEM((2, GROUPS - 1, OWN_ROWS, COLS), BF16),
            VMEM((2, PLEN, COLS), BF16),
            VMEM((ROWS, ROWS), F32),
            VMEM((HEADS, 768, 256), F32),
            VMEM((HEADS, 768, 256), F32),
            VMEM((HEADS, 2, PLEN, 256), F32),
            VMEM((HEADS, 2, PLEN, 256), BF16),
            VMEM((HEADS, 2, 8, 256), F32),
            VMEM((BATCHES, NY, PLEN, HS), BF16),
            VMEM((BATCHES, 2 * NY * GROUPS, OWN_ROWS, HS), BF16),
            VMEM((BATCHES, NZ, GROUPS, 16, HS), BF16),
            VMEM((BATCHES, NZ - 1, GROUPS, 16, HS), BF16),
            sem,
            sem((2, GROUPS)),
            sem((5,)),
        ]
        + pair(2, GROUPS - 1)
        + pair(BATCHES)
        + pair(BATCHES)
        + pair(BATCHES)
        + [sem((BATCHES,)), sem((BATCHES, NY - 1))]
        + pair(BATCHES),
        compiler_params=pltpu.CompilerParams(
            collective_id=1, has_side_effects=True, vmem_limit_bytes=VMEM_BYTES
        ),
        name="tree_grads",
    )(words, q, k, v, o, g, prefix_k, prefix_v)


def write_kernel(dq, dk, dv, sums_k, sums_v, dq_out, dk_out, dv_out, key_out, value_out, sems):
    pairs = [(dq, dq_out), (dk, dk_out), (dv, dv_out)]
    for sums, out in ((sums_k, key_out), (sums_v, value_out)):
        pairs += [(sums.at[xx], out.at[:, :, pl.ds(xx * COLS, COLS)]) for xx in range(GROUPS)]
    copies = [pltpu.make_async_copy(src, dst, sems.at[i]) for i, (src, dst) in enumerate(pairs)]
    for copy in copies:
        copy.start()
    for copy in copies:
        copy.wait()


def write(dq, dk, dv, sums_k, sums_v):
    big = jax.ShapeDtypeStruct((ROWS, COLS), BF16)
    small = jax.ShapeDtypeStruct((PROMPTS, OWN_ROWS, GROUPS * COLS), BF16)
    return pl.pallas_call(
        write_kernel,
        out_shape=(big, big, big, small, small),
        in_specs=[pl.BlockSpec(memory_space=VMEM)] * 5,
        out_specs=(pl.BlockSpec(memory_space=pltpu.HBM),) * 5,
        scratch_shapes=[pltpu.SemaphoreType.DMA((3 + 2 * GROUPS,))],
        compiler_params=pltpu.CompilerParams(vmem_limit_bytes=1 << 20),
        name="write",
    )(dq, dk, dv, sums_k, sums_v)


def per_device(q, k, v, o, g, prefix_k, prefix_v, parents, lengths, prompt_of):
    words = jnp.concatenate([prompt_of[:, 0], parents[0], lengths[0]])
    return write(*fused(words, q, k, v, o, g, prefix_k, prefix_v))


def solution(mesh):
    split = P("br", "hd")
    held = P(None, "hd", None)
    return jax.shard_map(
        per_device,
        mesh=mesh,
        in_specs=(split,) * 5 + (held, held, P("br", None), P("br", None), P()),
        out_specs=(split,) * 3 + (held, held),
        check_vma=False,
    )
```
